256 devices in a mesh: section: 4 (over y_lo, core), dp: 4 (over x), expert: 16 (over z, y_hi).
Axes of the slice: x: 4, y: 4 (y_hi: 2, y_lo: 2; y = y_hi * 2 + y_lo), z: 8, core: 2. Of those that a mesh axis runs over, the one named last changes fastest.
Arguments:
- inbound: bfloat16 [32768, 2048], P(('section', 'dp', 'expert')), may hold values from -6 to 6
- expert_ids: int32 [32768, 1], P(('section', 'dp', 'expert')), may hold values from 0 to 3
- gates: float32 [32768, 1], P(('section', 'dp', 'expert')), may hold values from 0.2 to 1
- w_in: bfloat16 [4, 2048, 8192], P('section', None, 'expert'), may hold values from -0.125 to 0.125
- w_out: bfloat16 [4, 8192, 2048], P('section', 'expert'), may hold values from -0.0625 to 0.0625
- mlp_in: bfloat16 [2048, 8192], P(None, 'expert'), may hold values from -0.125 to 0.125
- mlp_out: bfloat16 [8192, 2048], P('expert'), may hold values from -0.0625 to 0.0625
Outputs:
- mixed: bfloat16 [32768, 2048], P(('section', 'dp', 'expert'))
The draws below stay inside these ranges and needn't reach their ends.
All inputs are finite; a program needn't handle non-finite values.
Results may differ from the reference program's by a relative error of at most 0.02.
Values may be sent and summed in bfloat16 or wider, within the bound.
A program may use at most 128 MiB of HBM per device.

```python
import jax
import jax.numpy as jnp
from jax import lax

D = 2048
FF = 8192
TOK_DEV = 128
CAP = 20
EXPERTS = 4
TOKENS = 32768
N_SECTION = 4
N_EXPERT = 16


def level_of(own_key, dims, cuts, smallest, top_value):
    loudness = 1.0
    for dim, parts in cuts:
        heights = jax.random.uniform(jax.random.fold_in(jax.random.fold_in(own_key, 6), dim), (parts,), jnp.float32, smallest / len(cuts), top_value / len(cuts))
        loudness = loudness * jnp.repeat(jnp.exp(heights), dims[dim] // parts).reshape((-1,) + (1,) * (len(dims) - 1 - dim))
    return loudness


def different_ones(key, rows, number_of, top, lift):
    ranking = jax.random.permutation(jax.random.fold_in(key, 1), number_of)
    pull = ranking
    for power in range(3):
        pull = pull * pull // number_of
    pull = pull * lift // number_of
    tickets = jax.random.randint(jax.random.fold_in(key, 2), (rows, number_of), 0, 4096) + pull
    holders = jax.random.permutation(jax.random.fold_in(key, 3), rows)[jnp.arange(number_of) % rows]
    tickets = jnp.where(jnp.arange(rows)[:, None] == holders[None, :], 1 << 14, tickets)
    score = tickets * number_of + jnp.arange(number_of)
    return lax.top_k(score.astype(jnp.int32), top)[1].astype(jnp.int32)


def bell_draw(key, shape, deviation, reach, cuts=(), kind=jnp.bfloat16):
    result = deviation * jax.random.normal(key, shape, jnp.float32)
    if cuts:
        result = result * level_of(key, shape, cuts, -0.22, 0.18)
    return jnp.clip(result, -reach, reach).astype(kind)


def setup_inputs(seed: int = 0) -> dict:
    arg_keys = jax.random.split(jax.random.key(seed), 8)
    inbound = bell_draw(arg_keys[0], (TOKENS, D), 1.0, 6.0, ((0, 256),))
    expert_ids = different_ones(arg_keys[1], TOKENS, EXPERTS, 1, 2048)
    gates = jnp.clip(0.2 + 0.8 * jax.random.uniform(arg_keys[2], (TOKENS, 1), jnp.float32) ** level_of(arg_keys[2], (TOKENS, 1), ((0, 256),), -0.2, 0.2), 0.2, 1.0)
    w_in = bell_draw(arg_keys[3], (EXPERTS, D, FF), D ** -0.5, 0.125, ((0, 4), (2, 16)))
    w_out = bell_draw(arg_keys[4], (EXPERTS, FF, D), FF ** -0.5, 0.0625, ((0, 4), (1, 16)))
    mlp_in = bell_draw(arg_keys[5], (D, FF), D ** -0.5, 0.125, ((1, 16),))
    mlp_out = bell_draw(arg_keys[6], (FF, D), FF ** -0.5, 0.0625, ((0, 16),))
    return {"inbound": inbound, "expert_ids": expert_ids, "gates": gates, "w_in": w_in, "w_out": w_out, "mlp_in": mlp_in, "mlp_out": mlp_out}


def activate(rows, weights):
    return jax.nn.gelu(jnp.dot(rows, weights, preferred_element_type=jnp.float32), approximate=True).astype(jnp.bfloat16)


def grouped_sum(hidden, weight):
    width = FF // N_EXPERT

    def step(total, index):
        columns = lax.dynamic_slice_in_dim(hidden, index * width, width, 1)
        rows = lax.dynamic_slice_in_dim(weight, index * width, width, 0)
        part = jnp.dot(columns, rows, preferred_element_type=jnp.float32).astype(jnp.bfloat16)
        part = lax.optimization_barrier(part)
        return total + part.astype(jnp.float32), None

    start = jnp.zeros((hidden.shape[0], weight.shape[1]), jnp.float32)
    total, _ = lax.scan(step, start, jnp.arange(N_EXPERT, dtype=jnp.int32))
    return total


def run_expert(inputs_one):
    rows, weight_in, weight_out = inputs_one
    hidden = activate(rows, weight_in)
    return grouped_sum(hidden, weight_out).astype(jnp.bfloat16)


def reference(inbound, expert_ids, gates, w_in, w_out, mlp_in, mlp_out):
    section_rows = TOKENS // N_SECTION
    devices_all = TOKENS // TOK_DEV
    moved = jnp.roll(inbound, section_rows, axis=0)
    chosen = expert_ids[:, 0]
    blocks = chosen.reshape(devices_all, TOK_DEV)
    onehot = (blocks[:, :, None] == jnp.arange(EXPERTS, dtype=jnp.int32)[None, None, :]).astype(jnp.int32)
    before = jnp.cumsum(onehot, axis=1) - onehot
    position = jnp.sum(before * onehot, axis=2).reshape(-1)
    kept_mask = position < CAP
    owner_device = jnp.arange(TOKENS, dtype=jnp.int32) // TOK_DEV
    slot_index = jnp.where(kept_mask, owner_device * CAP + position, devices_all * CAP).astype(jnp.int32)
    buffer = jnp.zeros((EXPERTS, devices_all * CAP, D), jnp.bfloat16)
    buffer = buffer.at[chosen, slot_index].set(moved, mode="drop")
    results = lax.map(run_expert, (buffer, w_in, w_out))
    picked = results[chosen, jnp.minimum(slot_index, devices_all * CAP - 1)].astype(jnp.float32)
    expert_part = jnp.where(kept_mask[:, None], picked, jnp.float32(0.0))
    dense_hidden = activate(moved, mlp_in)
    dense_out = grouped_sum(dense_hidden, mlp_out)
    return (dense_out + gates * expert_part).astype(jnp.bfloat16)
```

```python
import functools

import jax
import jax.numpy as jnp
from jax import lax
from jax.experimental import pallas as pl
from jax.experimental.pallas import tpu as pltpu
from jax.sharding import PartitionSpec as P

MESH = pl.DeviceIdType.MESH
F32 = jnp.float32
BF16 = jnp.bfloat16
ROWS = 128
HALF = 64
CAP = 20
SLOT = 48
COLS = 256


def relayed_experts(
    ids_ref, gates_ref, inbound, w_in, w_out, mlp_in, mlp_out, out_ref,
    own_in, own_out, far_in, far_out, eown_in, eown_out, efar_in, efar_out,
    x, info, picked, rows, hid, ehid, dense, leaving, back, rs_out, rs_in,
    local_sem, hand_s, hand_r, info_s, info_r, ag_s, ag_r, w1_s, w1_r, w2_s, w2_r,
    core_s, core_r, disp_s, disp_r, ret_s, ret_r, rs_s, rs_r,
):
    s, d, e = lax.axis_index("section"), lax.axis_index("dp"), lax.axis_index("expert")
    core = lax.rem(s, 2)
    flip_e = e + 1 - 2 * lax.rem(e, 2)

    def along_z(k):
        return (s, d, lax.rem(e + 2 * (k % 8), 16))

    def at_section(k):
        return (lax.rem(s + k % 4, 4), d, e)

    def along_x(k):
        return (s, lax.rem(d + k % 4, 4), e)

    other_core = (s + 1 - 2 * core, d, e)
    far_expert = (s, d, flip_e)
    far_mlp = (lax.rem(s + 2, 4), d, flip_e)

    barrier = pltpu.get_barrier_semaphore()
    partners = [along_z(k) for k in range(1, 8)] + [at_section(k) for k in (1, 2, 3)]
    partners += [along_x(1), along_x(3), far_expert, far_mlp]
    for partner in partners:
        pl.semaphore_signal(barrier, inc=1, device_id=partner, device_id_type=MESH)

    local = [
        pltpu.make_async_copy(src, dst, local_sem.at[i])
        for i, (src, dst) in enumerate(
            [(mlp_in, own_in), (mlp_out, own_out), (w_in, eown_in), (w_out, eown_out)]
        )
    ]
    for copy in local:
        copy.start()
    pl.semaphore_wait(barrier, len(partners))

    sent = []

    def send(src, dst, send_sem, recv_sem, device):
        copy = pltpu.make_async_remote_copy(
            src_ref=src, dst_ref=dst, send_sem=send_sem, recv_sem=recv_sem,
            device_id=device, device_id_type=MESH,
        )
        copy.start()
        sent.append(copy)

    def arrived(dst, send_sem, recv_sem, device):
        pltpu.make_async_remote_copy(
            src_ref=dst, dst_ref=dst, send_sem=send_sem, recv_sem=recv_sem,
            device_id=device, device_id_type=MESH,
        ).wait_recv()

    for c in range(2):
        part = pl.ds(c * HALF, HALF)
        send(inbound.at[part], x.at[3, part], hand_s.at[c], hand_r.at[c], at_section(1))

    streams = [
        (mlp_in, far_in, 256, core * 1024, far_mlp),
        (mlp_out, far_out, 64, core * 256, far_mlp),
        (w_in, efar_in, 512, 0, far_expert),
        (w_out, efar_out, 128, 0, far_expert),
    ]

    def quarter(i, ref, k, part=None):
        _, _, q, base, _ = streams[i]
        first = base + lax.rem(d + k % 4, 4) * q
        if part is None:
            return ref.at[pl.ds(pl.multiple_of(first, 64), q)]
        return ref.at[pl.ds(pl.multiple_of(first + part * (q // 2), 32), q // 2)]

    def leg1(i):
        src, dst, _, _, device = streams[i]
        send(quarter(i, src, 0), quarter(i, dst, 0), w1_s.at[i], w1_r.at[i], device)

    def leg2(i):
        dst, device = streams[i][1], streams[i][4]
        mine = quarter(i, dst, 0)
        arrived(mine, w1_s.at[i], w1_r.at[i], device)
        send(mine, mine, w2_s.at[i, 0], w2_r.at[i, 0], along_x(1))
        send(mine, mine, w2_s.at[i, 1], w2_r.at[i, 1], along_x(3))

    def leg3(i):
        dst = streams[i][1]
        arrived(quarter(i, dst, 3), w2_s.at[i, 0], w2_r.at[i, 0], along_x(3))
        part = quarter(i, dst, 3, 0)
        send(part, part, w2_s.at[i, 2], w2_r.at[i, 2], along_x(1))
        arrived(quarter(i, dst, 1), w2_s.at[i, 1], w2_r.at[i, 1], along_x(1))
        part = quarter(i, dst, 1, 1)
        send(part, part, w2_s.at[i, 3], w2_r.at[i, 3], along_x(3))

    def leg4(i):
        dst = streams[i][1]
        arrived(quarter(i, dst, 2, 0), w2_s.at[i, 2], w2_r.at[i, 2], along_x(3))
        arrived(quarter(i, dst, 2, 1), w2_s.at[i, 3], w2_r.at[i, 3], along_x(1))

    def mlp_half(i, side):
        dst = streams[i][1]
        n = streams[i][2] * 4
        return dst.at[pl.ds(pl.multiple_of(side * n, 64), n)]

    leg1(0)
    leg1(1)
    leg1(2)

    ids = jnp.broadcast_to(ids_ref[...].astype(F32), (ROWS, ROWS))
    earlier = lax.broadcasted_iota(jnp.int32, (ROWS, ROWS), 0)
    token = lax.broadcasted_iota(jnp.int32, (ROWS, ROWS), 1)
    same = jnp.where((ids.T == ids) & (earlier < token), 1.0, 0.0)
    position = jnp.sum(same, axis=0, keepdims=True)
    relative = ids_ref[...] - s
    relative = jnp.where(relative < 0, relative + 4, relative).astype(F32)
    code = jnp.where(position < CAP, relative * SLOT + position, -1000.0)
    line = lax.broadcasted_iota(jnp.int32, (8, ROWS), 0)
    info[0] = jnp.where(
        line == 0,
        jnp.broadcast_to(code, (8, ROWS)),
        jnp.broadcast_to(gates_ref[...], (8, ROWS)),
    )
    for k in range(1, 8):
        send(info.at[0], info.at[k], info_s.at[k], info_r.at[k], along_z(k))

    step = (1, -1)

    def place(direction, hop, c):
        if hop == 4:
            return x.at[3, pl.ds(ROWS + c * HALF, HALF)]
        return x.at[hop - 1, pl.ds(direction * ROWS + c * HALF, HALF)]

    def chunks(direction):
        return (0, 1) if direction == 0 else (1, 0)

    def hop_out(direction, hop, c, src):
        send(
            src, place(direction, hop, c),
            ag_s.at[direction, hop - 1, c], ag_r.at[direction, hop - 1, c],
            along_z(step[direction]),
        )

    def hop_in(hop):
        for i in range(2 if hop < 4 else 1):
            for direction in range(2):
                c = chunks(direction)[i]
                dst = place(direction, hop, c)
                arrived(
                    dst, ag_s.at[direction, hop - 1, c], ag_r.at[direction, hop - 1, c],
                    along_z(-step[direction]),
                )
                if hop < 3 or (hop == 3 and i == 0):
                    hop_out(direction, hop + 1, c, dst)

    for c in range(2):
        own = x.at[3, pl.ds(c * HALF, HALF)]
        arrived(own, hand_s.at[c], hand_r.at[c], at_section(3))
        for direction in range(2):
            hop_out(direction, 1, c, own)
    leg1(3)

    sources = [(1, 7), (2, 6), (3, 5), (0, 4)]

    def placing(g, weighted):
        parts = []
        for side, k in enumerate(sources[g]):
            slot = lax.broadcasted_iota(jnp.int32, (4 * SLOT, ROWS), 0).astype(F32)
            want = info[k, 0:1, :] + float(side * CAP)
            value = info[k, 1:2, :] if weighted else 1.0
            parts.append(jnp.where(slot == want, value, 0.0))
        return jnp.concatenate(parts, axis=1).astype(BF16)

    def tiles(n, body):
        def run(i, _):
            body(pl.ds(pl.multiple_of(i * COLS, COLS), COLS))
            return 0

        lax.fori_loop(0, n // COLS, run, 0)

    def dispatch(g):
        for k in sources[g]:
            if k:
                arrived(info.at[k], info_s.at[k], info_r.at[k], along_z(-k))
        pick = placing(g, False)

        def body(cols):
            got = jnp.dot(pick, x[g, :, cols], preferred_element_type=F32).astype(BF16)
            rows[g, 0:SLOT, cols] = got[0:SLOT]
            picked[g, :, cols] = got[SLOT:]

        tiles(2048, body)
        for k in (2, 3, 1):
            send(
                picked.at[g, pl.ds((k - 1) * SLOT, SLOT)], rows.at[g, pl.ds(k * SLOT, SLOT)],
                disp_s.at[g, k], disp_r.at[g, k], at_section(k),
            )

    def dispatched(g):
        for k in (1, 2, 3):
            arrived(
                rows.at[g, pl.ds(k * SLOT, SLOT)], disp_s.at[g, k], disp_r.at[g, k], at_section(-k)
            )

    def first(src, weight, dst, g, offset):
        def run(i, _):
            cols = pl.ds(pl.multiple_of(i * COLS, COLS), COLS)
            to = pl.ds(pl.multiple_of(offset + i * COLS, COLS), COLS)
            dst[g, :, to] = jax.nn.gelu(
                jnp.dot(src[g], weight[:, cols], preferred_element_type=F32), approximate=True
            ).astype(BF16)
            return 0

        lax.fori_loop(0, 512 // COLS, run, 0)

    def dense_second(g):
        def body(cols):
            dense[g, :, cols] = jnp.dot(
                hid[g, :, 0:512], own_out[:, cols], preferred_element_type=F32
            ) + jnp.dot(hid[g, :, 512:1024], far_out[:, cols], preferred_element_type=F32)

        tiles(2048, body)

    def expert_second(g):
        def body(cols):
            got = jnp.dot(ehid[g, :, 0:512], eown_out[:, cols], preferred_element_type=F32)
            got += jnp.dot(ehid[g, :, 512:1024], efar_out[:, cols], preferred_element_type=F32)
            got = got.astype(BF16)
            back[g, 0:SLOT, cols] = got[0:SLOT]
            leaving[g, :, cols] = got[SLOT:]

        tiles(2048, body)
        for k in (2, 3, 1):
            send(
                leaving.at[g, pl.ds((k - 1) * SLOT, SLOT)], back.at[g, pl.ds(k * SLOT, SLOT)],
                ret_s.at[g, k], ret_r.at[g, k], at_section(-k),
            )

    def combine(g):
        for k in (1, 2, 3):
            arrived(
                back.at[g, pl.ds(k * SLOT, SLOT)], ret_s.at[g, k], ret_r.at[g, k], at_section(k)
            )
        put = placing(g, True)

        def body(cols):
            dense[g, :, cols] += lax.dot_general(
                put, back[g, :, cols], (((0,), (0,)), ((), ())), preferred_element_type=F32
            )

        tiles(2048, body)

    for copy in local:
        copy.wait()
    leg2(0)
    leg2(1)
    hop_in(1)
    dispatch(0)
    first(x, own_in, hid, 0, 0)
    leg2(2)
    hop_in(2)
    dispatch(1)
    leg2(3)
    first(x, own_in, hid, 1, 0)
    dispatched(0)
    first(rows, eown_in, ehid, 0, 0)
    leg3(0)
    leg3(1)
    hop_in(3)
    dispatch(2)
    first(x, own_in, hid, 2, 0)
    dispatched(1)
    first(rows, eown_in, ehid, 1, 0)
    leg4(0)
    leg4(1)
    for i in range(2):
        half = mlp_half(i, core)
        send(half, half, core_s.at[i], core_r.at[i], other_core)
    hop_in(4)
    dispatch(3)
    first(x, own_in, hid, 3, 0)
    leg3(2)
    leg3(3)
    for i in range(2):
        arrived(mlp_half(i, 1 - core), core_s.at[i], core_r.at[i], other_core)
    for g in (3, 2, 1, 0):
        first(x, far_in, hid, g, 512)
        dense_second(g)
    dispatched(2)
    first(rows, eown_in, ehid, 2, 0)
    dispatched(3)
    first(rows, eown_in, ehid, 3, 0)
    leg4(2)
    leg4(3)
    for g in (3, 2, 1, 0):
        first(rows, efar_in, ehid, g, 512)
        expert_second(g)

    def passing(direction, hop, c):
        if hop == 4:
            return 3, pl.ds(ROWS + c * HALF, HALF)
        return hop - 1, pl.ds((1 - direction) * ROWS + c * HALF, HALF)

    combine(3)
    for hop in (4, 3, 2, 1):
        for i in range(1 if hop == 4 else 2):
            for direction in range(2):
                c = chunks(direction)[i]
                g, where = passing(direction, hop, c)
                mine = rs_out.at[direction, hop - 1, pl.ds(c * HALF, HALF)]
                total = dense[g, where, :]
                if hop < 3 or (hop == 3 and i == 0):
                    before = rs_in.at[direction, hop, pl.ds(c * HALF, HALF)]
                    arrived(
                        before, rs_s.at[direction, hop, c], rs_r.at[direction, hop, c],
                        along_z(-step[direction]),
                    )
                    total = total + before[...].astype(F32)
                mine[...] = total.astype(BF16)
                send(
                    mine, rs_in.at[direction, hop - 1, pl.ds(c * HALF, HALF)],
                    rs_s.at[direction, hop - 1, c], rs_r.at[direction, hop - 1, c],
                    along_z(step[direction]),
                )
        if hop > 1:
            combine(hop - 2)
    for c in range(2):
        part = pl.ds(c * HALF, HALF)
        total = dense[3, part, :]
        for direction in range(2):
            before = rs_in.at[direction, 0, part]
            arrived(
                before, rs_s.at[direction, 0, c], rs_r.at[direction, 0, c], along_z(-step[direction])
            )
            total = total + before[...].astype(F32)
        out_ref[part, :] = total.astype(BF16)

    for copy in sent:
        copy.wait_send()


def solution(mesh):
    def shards(inbound, expert_ids, gates, w_in, w_out, mlp_in, mlp_out):
        vmem, dma = pltpu.VMEM, pltpu.SemaphoreType.DMA
        return pl.pallas_call(
            relayed_experts,
            out_shape=jax.ShapeDtypeStruct((ROWS, 2048), BF16),
            in_specs=[pl.BlockSpec(memory_space=pltpu.VMEM)] * 2
            + [pl.BlockSpec(memory_space=pl.ANY)] * 5,
            out_specs=pl.BlockSpec(memory_space=pltpu.VMEM),
            scratch_shapes=[
                vmem((2048, 512), BF16), vmem((512, 2048), BF16),
                vmem((2048, 512), BF16), vmem((512, 2048), BF16),
                vmem((2048, 512), BF16), vmem((512, 2048), BF16),
                vmem((2048, 512), BF16), vmem((512, 2048), BF16),
                vmem((4, 2 * ROWS, 2048), BF16),
                vmem((8, 8, ROWS), F32),
                vmem((4, 3 * SLOT, 2048), BF16),
                vmem((4, 4 * SLOT, 2048), BF16),
                vmem((4, 2 * ROWS, 1024), BF16),
                vmem((4, 4 * SLOT, 1024), BF16),
                vmem((4, 2 * ROWS, 2048), F32),
                vmem((4, 3 * SLOT, 2048), BF16),
                vmem((4, 4 * SLOT, 2048), BF16),
                vmem((2, 4, ROWS, 2048), BF16),
                vmem((2, 4, ROWS, 2048), BF16),
                dma((4,)),
                dma((2,)), dma((2,)),
                dma((8,)), dma((8,)),
                dma((2, 4, 2)), dma((2, 4, 2)),
                dma((4,)), dma((4,)),
                dma((4, 4)), dma((4, 4)),
                dma((2,)), dma((2,)),
                dma((4, 4)), dma((4, 4)),
                dma((4, 4)), dma((4, 4)),
                dma((2, 4, 2)), dma((2, 4, 2)),
            ],
            compiler_params=pltpu.CompilerParams(
                collective_id=0, has_side_effects=True, vmem_limit_bytes=60 * 2**20
            ),
        )(
            expert_ids.reshape(1, ROWS), gates.reshape(1, ROWS), inbound,
            w_in[0], w_out[0], mlp_in, mlp_out,
        )

    return jax.shard_map(
        shards,
        mesh=mesh,
        in_specs=(
            P(("section", "dp", "expert"), None),
            P(("section", "dp", "expert"), None),
            P(("section", "dp", "expert"), None),
            P("section", None, "expert"),
            P("section", "expert", None),
            P(None, "expert"),
            P("expert", None),
        ),
        out_specs=P(("section", "dp", "expert"), None),
        check_vma=False,
    )
```

```python
import functools

import jax
import jax.numpy as jnp
from jax import lax
from jax.experimental import pallas as pl
from jax.experimental.pallas import tpu as pltpu
from jax.sharding import PartitionSpec as P

MESH = pl.DeviceIdType.MESH
F32 = jnp.float32
BF16 = jnp.bfloat16
ROWS = 128
HALF = 64
CAP = 20
BLOCKS = ((0, 1, 7), (2, 6), (3, 5), (4,))
TOKENS = tuple(len(group) * ROWS for group in BLOCKS)
TOKENS_AT = tuple(sum(TOKENS[:g]) for g in range(4))
SLOTS = (64, 48, 48, 32)
SLOTS_AT = tuple(4 * sum(SLOTS[:g]) for g in range(4))
PICKED_AT = tuple(3 * sum(SLOTS[:g]) for g in range(4))
BLOCK_AT = {k: TOKENS_AT[g] + i * ROWS for g in range(4) for i, k in enumerate(BLOCKS[g])}
COLS = 512


def relayed_experts(
    ids_ref, gates_ref, inbound, w_in, w_out, mlp_in, mlp_out, out_ref,
    own_in, own_out, far_in, far_out, eown_in, eown_out, efar_in, efar_out,
    x, info, picked, rows, hid, ehid, dense, leaving, back, rs_out, rs_in,
    local_sem, hand_s, hand_r, info_s, info_r, ag_s, ag_r, w1_s, w1_r, w2_s, w2_r,
    core_s, core_r, disp_s, disp_r, ret_s, ret_r, rs_s, rs_r,
):
    s, d, e = lax.axis_index("section"), lax.axis_index("dp"), lax.axis_index("expert")
    core = lax.rem(s, 2)
    flip_e = e + 1 - 2 * lax.rem(e, 2)

    def along_z(k):
        return (s, d, lax.rem(e + 2 * (k % 8), 16))

    def at_section(k):
        return (lax.rem(s + k % 4, 4), d, e)

    def along_x(k):
        return (s, lax.rem(d + k % 4, 4), e)

    other_core = (s + 1 - 2 * core, d, e)
    far_expert = (s, d, flip_e)
    far_mlp = (lax.rem(s + 2, 4), d, flip_e)

    barrier = pltpu.get_barrier_semaphore()
    partners = [along_z(k) for k in range(1, 8)] + [at_section(k) for k in (1, 2, 3)]
    partners += [along_x(1), along_x(3), far_expert, far_mlp]
    for partner in partners:
        pl.semaphore_signal(barrier, inc=1, device_id=partner, device_id_type=MESH)

    local = [
        pltpu.make_async_copy(src, dst, local_sem.at[i])
        for i, (src, dst) in enumerate(
            [(mlp_in, own_in), (mlp_out, own_out), (w_in, eown_in), (w_out, eown_out)]
        )
    ]
    for copy in local:
        copy.start()
    pl.semaphore_wait(barrier, len(partners))

    sent = []

    def send(src, dst, send_sem, recv_sem, device):
        copy = pltpu.make_async_remote_copy(
            src_ref=src, dst_ref=dst, send_sem=send_sem, recv_sem=recv_sem,
            device_id=device, device_id_type=MESH,
        )
        copy.start()
        sent.append(copy)

    def arrived(dst, send_sem, recv_sem, device):
        pltpu.make_async_remote_copy(
            src_ref=dst, dst_ref=dst, send_sem=send_sem, recv_sem=recv_sem,
            device_id=device, device_id_type=MESH,
        ).wait_recv()

    for c in range(2):
        part = pl.ds(c * HALF, HALF)
        send(inbound.at[part], x.at[part], hand_s.at[c], hand_r.at[c], at_section(1))

    streams = [
        (mlp_in, far_in, 256, core * 1024, far_mlp),
        None,
        (w_in, efar_in, 256, 0, far_expert),
        (w_out, efar_out, 64, 0, far_expert),
        (w_in, efar_in, 256, 1024, far_expert),
        (w_out, efar_out, 64, 256, far_expert),
    ]

    def quarter(i, ref, k, part=None):
        _, _, q, base, _ = streams[i]
        first = base + lax.rem(d + k % 4, 4) * q
        if part is None:
            return ref.at[pl.ds(pl.multiple_of(first, 64), q)]
        return ref.at[pl.ds(pl.multiple_of(first + part * (q // 2), 32), q // 2)]

    def leg1(i):
        src, dst, _, _, device = streams[i]
        send(quarter(i, src, 0), quarter(i, dst, 0), w1_s.at[i], w1_r.at[i], device)

    def leg2(i):
        dst, device = streams[i][1], streams[i][4]
        mine = quarter(i, dst, 0)
        arrived(mine, w1_s.at[i], w1_r.at[i], device)
        send(mine, mine, w2_s.at[i, 0], w2_r.at[i, 0], along_x(1))
        send(mine, mine, w2_s.at[i, 1], w2_r.at[i, 1], along_x(3))

    def leg3(i):
        dst = streams[i][1]
        arrived(quarter(i, dst, 3), w2_s.at[i, 0], w2_r.at[i, 0], along_x(3))
        part = quarter(i, dst, 3, 0)
        send(part, part, w2_s.at[i, 2], w2_r.at[i, 2], along_x(1))
        arrived(quarter(i, dst, 1), w2_s.at[i, 1], w2_r.at[i, 1], along_x(1))
        part = quarter(i, dst, 1, 1)
        send(part, part, w2_s.at[i, 3], w2_r.at[i, 3], along_x(3))

    def leg4(i):
        dst = streams[i][1]
        arrived(quarter(i, dst, 2, 0), w2_s.at[i, 2], w2_r.at[i, 2], along_x(3))
        arrived(quarter(i, dst, 2, 1), w2_s.at[i, 3], w2_r.at[i, 3], along_x(1))

    def mlp_half(i, ref, side):
        n = (1024, 256)[i]
        return ref.at[pl.ds(pl.multiple_of(side * n, 64), n)]

    def direct():
        src, dst = mlp_half(1, mlp_out, core), mlp_half(1, far_out, core)
        send(src, dst, w1_s.at[1], w1_r.at[1], far_mlp)

    def direct_in():
        arrived(mlp_half(1, far_out, core), w1_s.at[1], w1_r.at[1], far_mlp)

    def to_other_core(i):
        half = mlp_half(i, (far_in, far_out)[i], core)
        send(half, half, core_s.at[i], core_r.at[i], other_core)

    def from_other_core(i):
        arrived(mlp_half(i, (far_in, far_out)[i], 1 - core), core_s.at[i], core_r.at[i], other_core)

    leg1(0)

    ids = jnp.broadcast_to(ids_ref[...].astype(F32), (ROWS, ROWS))
    earlier = lax.broadcasted_iota(jnp.int32, (ROWS, ROWS), 0)
    token = lax.broadcasted_iota(jnp.int32, (ROWS, ROWS), 1)
    same = jnp.where((ids.T == ids) & (earlier < token), 1.0, 0.0)
    position = jnp.sum(same, axis=0, keepdims=True)
    relative = ids_ref[...] - s
    relative = jnp.where(relative < 0, relative + 4, relative).astype(F32)
    position = jnp.where(position < CAP, position, -1e6)
    line = lax.broadcasted_iota(jnp.int32, (8, ROWS), 0)
    info[0] = jnp.where(
        line == 0,
        jnp.broadcast_to(relative, (8, ROWS)),
        jnp.where(
            line == 1,
            jnp.broadcast_to(position, (8, ROWS)),
            jnp.broadcast_to(gates_ref[...], (8, ROWS)),
        ),
    )
    for k in range(1, 8):
        send(info.at[0], info.at[k], info_s.at[k], info_r.at[k], along_z(k))

    step = (1, -1)

    def block(direction, hop):
        return BLOCK_AT[hop if direction == 0 else 8 - hop]

    def place(direction, hop, c):
        return x.at[pl.ds(block(direction, hop) + c * HALF, HALF)]

    def chunks(direction):
        return (0, 1) if direction == 0 else (1, 0)

    def hop_out(direction, hop, c, src):
        send(
            src, place(direction, hop, c),
            ag_s.at[direction, hop - 1, c], ag_r.at[direction, hop - 1, c],
            along_z(step[direction]),
        )

    def hop_in(hop, i):
        for direction in range(2):
            c = chunks(direction)[i]
            dst = place(direction, hop, c)
            arrived(
                dst, ag_s.at[direction, hop - 1, c], ag_r.at[direction, hop - 1, c],
                along_z(-step[direction]),
            )
            if hop < 3 or (hop == 3 and i == 0):
                hop_out(direction, hop + 1, c, dst)

    for c in range(2):
        own = x.at[pl.ds(c * HALF, HALF)]
        arrived(own, hand_s.at[c], hand_r.at[c], at_section(3))
        for direction in range(2):
            hop_out(direction, 1, c, own)
        leg1((2, 4)[c])

    def placing(g):
        parts = []
        for side, k in enumerate(BLOCKS[g]):
            slot = lax.broadcasted_iota(jnp.int32, (4 * SLOTS[g], ROWS), 0).astype(F32)
            want = info[k, 0:1, :] * float(SLOTS[g]) + info[k, 1:2, :] + float(side * CAP)
            parts.append(jnp.where(slot == want, 1.0, 0.0))
        return jnp.concatenate(parts, axis=1).astype(BF16)

    def weighting(g):
        parts = []
        for side, k in enumerate(BLOCKS[g]):
            columns = info[k].T
            slot = lax.broadcasted_iota(jnp.int32, (ROWS, 4 * SLOTS[g]), 1).astype(F32)
            want = columns[:, 0:1] * float(SLOTS[g]) + columns[:, 1:2] + float(side * CAP)
            parts.append(jnp.where(slot == want, columns[:, 2:3], 0.0))
        return jnp.concatenate(parts, axis=0).astype(BF16)

    def of_group(g):
        return pl.ds(TOKENS_AT[g], TOKENS[g])

    def slots_of(g):
        return pl.ds(SLOTS_AT[g], 4 * SLOTS[g])

    def slot_rows(g, k):
        return pl.ds(SLOTS_AT[g] + k * SLOTS[g], SLOTS[g])

    def picked_rows(g, k):
        return pl.ds(PICKED_AT[g] + (k - 1) * SLOTS[g], SLOTS[g])

    def tiles(n, body):
        def run(i, _):
            body(pl.ds(pl.multiple_of(i * COLS, COLS), COLS))
            return 0

        lax.fori_loop(0, n // COLS, run, 0)

    def dispatch(g):
        for k in BLOCKS[g]:
            if k:
                arrived(info.at[k], info_s.at[k], info_r.at[k], along_z(-k))
        pick = placing(g)

        def body(cols):
            got = jnp.dot(pick, x[of_group(g), cols], preferred_element_type=F32).astype(BF16)
            rows[slot_rows(g, 0), cols] = got[0 : SLOTS[g]]
            picked[pl.ds(PICKED_AT[g], 3 * SLOTS[g]), cols] = got[SLOTS[g] :]

        tiles(2048, body)
        for k in (2, 3, 1):
            send(
                picked.at[picked_rows(g, k)], rows.at[slot_rows(g, k)],
                disp_s.at[g, k], disp_r.at[g, k], at_section(k),
            )

    def dispatched(g):
        for k in (1, 2, 3):
            arrived(rows.at[slot_rows(g, k)], disp_s.at[g, k], disp_r.at[g, k], at_section(-k))

    def first(src, weight, dst, where, offset):
        dst[where, offset : offset + 512] = jax.nn.gelu(
            jnp.dot(src[where, :], weight[...], preferred_element_type=F32), approximate=True
        ).astype(BF16)

    def dense_near_first(g):
        first(x, own_in, hid, of_group(g), 0)

    def dense_far_first(g):
        first(x, far_in, hid, of_group(g), 512)

    def expert_near_first(g):
        first(rows, eown_in, ehid, slots_of(g), 0)

    def expert_far_first(g):
        first(rows, efar_in, ehid, slots_of(g), 512)

    def dense_near(g):
        def body(cols):
            dense[of_group(g), cols] = jnp.dot(
                hid[of_group(g), 0:512], own_out[:, cols], preferred_element_type=F32
            )

        tiles(2048, body)

    def dense_far(g):
        def body(cols):
            dense[of_group(g), cols] += jnp.dot(
                hid[of_group(g), 512:1024], far_out[:, cols], preferred_element_type=F32
            )

        tiles(2048, body)

    def expert_second(g):
        def body(cols):
            near, far = ehid[slots_of(g), 0:512], ehid[slots_of(g), 512:1024]
            got = jnp.dot(near, eown_out[:, cols], preferred_element_type=F32)
            got += jnp.dot(far, efar_out[:, cols], preferred_element_type=F32)
            got = got.astype(BF16)
            back[slot_rows(g, 0), cols] = got[0 : SLOTS[g]]
            leaving[pl.ds(PICKED_AT[g], 3 * SLOTS[g]), cols] = got[SLOTS[g] :]

        tiles(2048, body)

    def give_back(g):
        for k in (2, 3, 1):
            send(
                leaving.at[picked_rows(g, k)], back.at[slot_rows(g, k)],
                ret_s.at[g, k], ret_r.at[g, k], at_section(-k),
            )

    def combine(g):
        for k in (1, 2, 3):
            arrived(back.at[slot_rows(g, k)], ret_s.at[g, k], ret_r.at[g, k], at_section(k))
        put = weighting(g)

        def body(cols):
            dense[of_group(g), cols] += jnp.dot(
                put, back[slots_of(g), cols], preferred_element_type=F32
            )

        tiles(2048, body)

    leg2(0)
    for copy in local:
        copy.wait()
    hop_in(1, 0)
    leg2(2)
    leg1(3)
    hop_in(1, 1)
    leg2(4)
    leg1(5)
    dense_near_first(0)
    leg3(2)
    hop_in(2, 0)
    dispatch(0)
    leg2(3)
    leg3(4)
    hop_in(2, 1)
    leg2(5)
    direct()
    dispatch(1)
    dense_near(0)
    leg4(2)
    hop_in(3, 0)
    leg3(3)
    leg4(4)
    dense_near_first(1)
    hop_in(3, 1)
    dispatch(2)
    leg3(5)
    leg3(0)
    dense_near_first(2)
    hop_in(4, 0)
    dispatch(3)
    dense_near(2)
    leg4(3)
    dense_near_first(3)
    dense_near(1)
    dispatched(2)
    expert_near_first(2)
    expert_far_first(2)
    leg4(5)
    expert_second(2)
    give_back(2)
    leg4(0)
    to_other_core(0)
    direct_in()
    to_other_core(1)
    dispatched(3)
    expert_near_first(3)
    expert_far_first(3)
    expert_second(3)
    from_other_core(0)
    dense_far_first(2)
    from_other_core(1)
    dense_far(2)
    dense_far_first(3)
    dense_near(3)
    dense_far(3)

    def passing(direction, hop, c):
        return pl.ds(block(1 - direction, hop) + c * HALF, HALF)

    def hop_back(hop, i):
        for direction in range(2):
            c = chunks(direction)[i]
            mine = rs_out.at[direction, hop - 1, pl.ds(c * HALF, HALF)]
            total = dense[passing(direction, hop, c), :]
            if hop < 3 or (hop == 3 and i == 0):
                before = rs_in.at[direction, hop, pl.ds(c * HALF, HALF)]
                arrived(
                    before, rs_s.at[direction, hop, c], rs_r.at[direction, hop, c],
                    along_z(-step[direction]),
                )
                total = total + before[...].astype(F32)
            mine[...] = total.astype(BF16)
            send(
                mine, rs_in.at[direction, hop - 1, pl.ds(c * HALF, HALF)],
                rs_s.at[direction, hop - 1, c], rs_r.at[direction, hop - 1, c],
                along_z(step[direction]),
            )

    combine(2)
    give_back(3)
    hop_back(3, 1)
    dispatched(1)
    expert_near_first(1)
    expert_far_first(1)
    expert_second(1)
    combine(3)
    give_back(1)
    hop_back(4, 0)
    dispatched(0)
    expert_near_first(0)
    expert_far_first(0)
    expert_second(0)
    dense_far_first(1)
    dense_far(1)
    hop_back(3, 0)
    combine(1)
    give_back(0)
    hop_back(2, 1)
    dense_far_first(0)
    hop_back(2, 0)
    dense_far(0)
    combine(0)
    hop_back(1, 1)
    hop_back(1, 0)
    for c in range(2):
        part = pl.ds(c * HALF, HALF)
        total = dense[part, :]
        for direction in (c, 1 - c):
            before = rs_in.at[direction, 0, part]
            arrived(
                before, rs_s.at[direction, 0, c], rs_r.at[direction, 0, c], along_z(-step[direction])
            )
            total = total + before[...].astype(F32)
        out_ref[part, :] = total.astype(BF16)

    for copy in sent:
        copy.wait_send()


def solution(mesh):
    def shards(inbound, expert_ids, gates, w_in, w_out, mlp_in, mlp_out):
        vmem, dma = pltpu.VMEM, pltpu.SemaphoreType.DMA
        return pl.pallas_call(
            relayed_experts,
            out_shape=jax.ShapeDtypeStruct((ROWS, 2048), BF16),
            in_specs=[pl.BlockSpec(memory_space=pltpu.VMEM)] * 2
            + [pl.BlockSpec(memory_space=pl.ANY)] * 5,
            out_specs=pl.BlockSpec(memory_space=pltpu.VMEM),
            scratch_shapes=[
                vmem((2048, 512), BF16), vmem((512, 2048), BF16),
                vmem((2048, 512), BF16), vmem((512, 2048), BF16),
                vmem((2048, 512), BF16), vmem((512, 2048), BF16),
                vmem((2048, 512), BF16), vmem((512, 2048), BF16),
                vmem((8 * ROWS, 2048), BF16),
                vmem((8, 8, ROWS), F32),
                vmem((3 * sum(SLOTS), 2048), BF16),
                vmem((4 * sum(SLOTS), 2048), BF16),
                vmem((8 * ROWS, 1024), BF16),
                vmem((4 * sum(SLOTS), 1024), BF16),
                vmem((8 * ROWS, 2048), F32),
                vmem((3 * sum(SLOTS), 2048), BF16),
                vmem((4 * sum(SLOTS), 2048), BF16),
                vmem((2, 4, ROWS, 2048), BF16),
                vmem((2, 4, ROWS, 2048), BF16),
                dma((4,)),
                dma((2,)), dma((2,)),
                dma((8,)), dma((8,)),
                dma((2, 4, 2)), dma((2, 4, 2)),
                dma((6,)), dma((6,)),
                dma((6, 4)), dma((6, 4)),
                dma((2,)), dma((2,)),
                dma((4, 4)), dma((4, 4)),
                dma((4, 4)), dma((4, 4)),
                dma((2, 4, 2)), dma((2, 4, 2)),
            ],
            compiler_params=pltpu.CompilerParams(
                collective_id=0, has_side_effects=True, vmem_limit_bytes=60 * 2**20
            ),
        )(
            expert_ids.reshape(1, ROWS), gates.reshape(1, ROWS), inbound,
            w_in[0], w_out[0], mlp_in, mlp_out,
        )

    return jax.shard_map(
        shards,
        mesh=mesh,
        in_specs=(
            P(("section", "dp", "expert"), None),
            P(("section", "dp", "expert"), None),
            P(("section", "dp", "expert"), None),
            P("section", None, "expert"),
            P("section", "expert", None),
            P(None, "expert"),
            P("expert", None),
        ),
        out_specs=P(("section", "dp", "expert"), None),
        check_vma=False,
    )
```

```python
import functools

import jax
import jax.numpy as jnp
from jax import lax
from jax.experimental import pallas as pl
from jax.experimental.pallas import tpu as pltpu
from jax.sharding import PartitionSpec as P

MESH = pl.DeviceIdType.MESH
F32 = jnp.float32
BF16 = jnp.bfloat16
ROWS = 128
HALF = 64
CAP = 20
BLOCKS = ((0, 1, 7), (2, 6), (3, 5), (4,))
TOKENS = tuple(len(group) * ROWS for group in BLOCKS)
TOKENS_AT = tuple(sum(TOKENS[:g]) for g in range(4))
SLOTS = (64, 48, 48, 32)
SLOTS_AT = tuple(4 * sum(SLOTS[:g]) for g in range(4))
PICKED_AT = tuple(3 * sum(SLOTS[:g]) for g in range(4))
FAR_SIDE = (1,)
BLOCK_AT = {k: TOKENS_AT[g] + i * ROWS for g in range(4) for i, k in enumerate(BLOCKS[g])}
COLS = 512


def relayed_experts(
    ids_ref, gates_ref, inbound, w_in, w_out, mlp_in, mlp_out, out_ref,
    own_in, own_out, far_in, far_out, eown_in, eown_out, efar_in, efar_out,
    x, info, picked, rows, hid, ehid, dense, leaving, back, rs_out, rs_in,
    local_sem, hand_s, hand_r, info_s, info_r, ag_s, ag_r, w1_s, w1_r, w2_s, w2_r,
    core_s, core_r, disp_s, disp_r, ret_s, ret_r, rs_s, rs_r,
):
    s, d, e = lax.axis_index("section"), lax.axis_index("dp"), lax.axis_index("expert")
    core = lax.rem(s, 2)
    flip_e = e + 1 - 2 * lax.rem(e, 2)

    def along_z(k):
        return (s, d, lax.rem(e + 2 * (k % 8), 16))

    def at_section(k):
        return (lax.rem(s + k % 4, 4), d, e)

    def peer(g, k):
        t, _, _ = at_section(k)
        if g in FAR_SIDE:
            return (t, d, jnp.where(t // 2 == s // 2, e, flip_e))
        return (t, d, e)

    def along_x(k):
        return (s, lax.rem(d + k % 4, 4), e)

    other_core = (s + 1 - 2 * core, d, e)
    far_expert = (s, d, flip_e)
    far_mlp = (lax.rem(s + 2, 4), d, flip_e)

    barrier = pltpu.get_barrier_semaphore()
    partners = [along_z(k) for k in range(1, 8)] + [at_section(k) for k in (1, 2, 3)]
    partners += [(lax.rem(s + 3 - 2 * core, 4), d, flip_e), along_x(1), along_x(3), far_expert, far_mlp]
    for partner in partners:
        pl.semaphore_signal(barrier, inc=1, device_id=partner, device_id_type=MESH)

    local = [
        pltpu.make_async_copy(src, dst, local_sem.at[i])
        for i, (src, dst) in enumerate(
            [(mlp_in, own_in), (mlp_out, own_out), (w_in, eown_in), (w_out, eown_out)]
        )
    ]
    for copy in local:
        copy.start()
    pl.semaphore_wait(barrier, len(partners))

    sent = []

    def send(src, dst, send_sem, recv_sem, device):
        copy = pltpu.make_async_remote_copy(
            src_ref=src, dst_ref=dst, send_sem=send_sem, recv_sem=recv_sem,
            device_id=device, device_id_type=MESH,
        )
        copy.start()
        sent.append(copy)

    def arrived(dst, send_sem, recv_sem, device):
        pltpu.make_async_remote_copy(
            src_ref=dst, dst_ref=dst, send_sem=send_sem, recv_sem=recv_sem,
            device_id=device, device_id_type=MESH,
        ).wait_recv()

    for c in range(2):
        part = pl.ds(c * HALF, HALF)
        send(inbound.at[part], x.at[part], hand_s.at[c], hand_r.at[c], at_section(1))

    streams = [
        (mlp_out, far_out, 64, core * 256, far_mlp),
        None,
        (w_in, efar_in, 256, 0, far_expert),
        (w_out, efar_out, 64, 0, far_expert),
        (w_in, efar_in, 256, 1024, far_expert),
        (w_out, efar_out, 64, 256, far_expert),
    ]

    def quarter(i, ref, k, part=None):
        _, _, q, base, _ = streams[i]
        first = base + lax.rem(d + k % 4, 4) * q
        if part is None:
            return ref.at[pl.ds(pl.multiple_of(first, 64), q)]
        return ref.at[pl.ds(pl.multiple_of(first + part * (q // 2), 32), q // 2)]

    def leg1(i):
        src, dst, _, _, device = streams[i]
        send(quarter(i, src, 0), quarter(i, dst, 0), w1_s.at[i], w1_r.at[i], device)

    def leg2(i):
        dst, device = streams[i][1], streams[i][4]
        mine = quarter(i, dst, 0)
        arrived(mine, w1_s.at[i], w1_r.at[i], device)
        send(mine, mine, w2_s.at[i, 0], w2_r.at[i, 0], along_x(1))
        send(mine, mine, w2_s.at[i, 1], w2_r.at[i, 1], along_x(3))

    def leg3(i):
        dst = streams[i][1]
        arrived(quarter(i, dst, 3), w2_s.at[i, 0], w2_r.at[i, 0], along_x(3))
        part = quarter(i, dst, 3, 0)
        send(part, part, w2_s.at[i, 2], w2_r.at[i, 2], along_x(1))
        arrived(quarter(i, dst, 1), w2_s.at[i, 1], w2_r.at[i, 1], along_x(1))
        part = quarter(i, dst, 1, 1)
        send(part, part, w2_s.at[i, 3], w2_r.at[i, 3], along_x(3))

    def leg4(i):
        dst = streams[i][1]
        arrived(quarter(i, dst, 2, 0), w2_s.at[i, 2], w2_r.at[i, 2], along_x(3))
        arrived(quarter(i, dst, 2, 1), w2_s.at[i, 3], w2_r.at[i, 3], along_x(1))

    def mlp_half(i, ref, side):
        n = (1024, 256)[i]
        return ref.at[pl.ds(pl.multiple_of(side * n, 64), n)]

    def direct():
        src, dst = mlp_half(0, mlp_in, core), mlp_half(0, far_in, core)
        send(src, dst, w1_s.at[1], w1_r.at[1], far_mlp)

    def direct_in():
        arrived(mlp_half(0, far_in, core), w1_s.at[1], w1_r.at[1], far_mlp)

    def to_other_core(i):
        half = mlp_half(i, (far_in, far_out)[i], core)
        send(half, half, core_s.at[i], core_r.at[i], other_core)

    def from_other_core(i):
        arrived(mlp_half(i, (far_in, far_out)[i], 1 - core), core_s.at[i], core_r.at[i], other_core)

    leg1(0)

    ids = jnp.broadcast_to(ids_ref[...].astype(F32), (ROWS, ROWS))
    earlier = lax.broadcasted_iota(jnp.int32, (ROWS, ROWS), 0)
    token = lax.broadcasted_iota(jnp.int32, (ROWS, ROWS), 1)
    same = jnp.where((ids.T == ids) & (earlier < token), 1.0, 0.0)
    position = jnp.sum(same, axis=0, keepdims=True)
    relative = ids_ref[...] - s
    relative = jnp.where(relative < 0, relative + 4, relative).astype(F32)
    position = jnp.where(position < CAP, position, -1e6)
    line = lax.broadcasted_iota(jnp.int32, (8, ROWS), 0)
    info[0] = jnp.where(
        line == 0,
        jnp.broadcast_to(relative, (8, ROWS)),
        jnp.where(
            line == 1,
            jnp.broadcast_to(position, (8, ROWS)),
            jnp.broadcast_to(gates_ref[...], (8, ROWS)),
        ),
    )
    for k in range(1, 8):
        send(info.at[0], info.at[k], info_s.at[k], info_r.at[k], along_z(k))

    step = (1, -1)

    def block(direction, hop):
        return BLOCK_AT[hop if direction == 0 else 8 - hop]

    def place(direction, hop, c):
        return x.at[pl.ds(block(direction, hop) + c * HALF, HALF)]

    def chunks(direction):
        return (0, 1) if direction == 0 else (1, 0)

    def hop_out(direction, hop, c, src):
        send(
            src, place(direction, hop, c),
            ag_s.at[direction, hop - 1, c], ag_r.at[direction, hop - 1, c],
            along_z(step[direction]),
        )

    def hop_in(hop, i):
        for direction in range(2):
            c = chunks(direction)[i]
            dst = place(direction, hop, c)
            arrived(
                dst, ag_s.at[direction, hop - 1, c], ag_r.at[direction, hop - 1, c],
                along_z(-step[direction]),
            )
            if hop < 3 or (hop == 3 and i == 0):
                hop_out(direction, hop + 1, c, dst)

    for c in range(2):
        own = x.at[pl.ds(c * HALF, HALF)]
        arrived(own, hand_s.at[c], hand_r.at[c], at_section(3))
        for direction in range(2):
            hop_out(direction, 1, c, own)
        leg1((2, 4)[c])

    def placing(g):
        parts = []
        for side, k in enumerate(BLOCKS[g]):
            slot = lax.broadcasted_iota(jnp.int32, (4 * SLOTS[g], ROWS), 0).astype(F32)
            want = info[k, 0:1, :] * float(SLOTS[g]) + info[k, 1:2, :] + float(side * CAP)
            parts.append(jnp.where(slot == want, 1.0, 0.0))
        return jnp.concatenate(parts, axis=1).astype(BF16)

    def weighting(g):
        parts = []
        for side, k in enumerate(BLOCKS[g]):
            columns = info[k].T
            slot = lax.broadcasted_iota(jnp.int32, (ROWS, 4 * SLOTS[g]), 1).astype(F32)
            want = columns[:, 0:1] * float(SLOTS[g]) + columns[:, 1:2] + float(side * CAP)
            parts.append(jnp.where(slot == want, columns[:, 2:3], 0.0))
        return jnp.concatenate(parts, axis=0).astype(BF16)

    def of_group(g):
        return pl.ds(TOKENS_AT[g], TOKENS[g])

    def slots_of(g):
        return pl.ds(SLOTS_AT[g], 4 * SLOTS[g])

    def slot_rows(g, k):
        return pl.ds(SLOTS_AT[g] + k * SLOTS[g], SLOTS[g])

    def picked_rows(g, k):
        return pl.ds(PICKED_AT[g] + (k - 1) * SLOTS[g], SLOTS[g])

    def tiles(n, body):
        def run(i, _):
            body(pl.ds(pl.multiple_of(i * COLS, COLS), COLS))
            return 0

        lax.fori_loop(0, n // COLS, run, 0)

    def dispatch(g):
        for k in BLOCKS[g]:
            if k:
                arrived(info.at[k], info_s.at[k], info_r.at[k], along_z(-k))
        pick = placing(g)

        def body(cols):
            got = jnp.dot(pick, x[of_group(g), cols], preferred_element_type=F32).astype(BF16)
            rows[slot_rows(g, 0), cols] = got[0 : SLOTS[g]]
            picked[pl.ds(PICKED_AT[g], 3 * SLOTS[g]), cols] = got[SLOTS[g] :]

        tiles(2048, body)
        for k in (2, 3, 1):
            send(
                picked.at[picked_rows(g, k)], rows.at[slot_rows(g, k)],
                disp_s.at[g, k], disp_r.at[g, k], peer(g, k),
            )

    def dispatched(g):
        for k in (1, 2, 3):
            arrived(rows.at[slot_rows(g, k)], disp_s.at[g, k], disp_r.at[g, k], peer(g, -k))

    def first(src, weight, dst, where, offset):
        dst[where, offset : offset + 512] = jax.nn.gelu(
            jnp.dot(src[where, :], weight[...], preferred_element_type=F32), approximate=True
        ).astype(BF16)

    def dense_near_first(g):
        first(x, own_in, hid, of_group(g), 0)

    def dense_far_first(g):
        first(x, far_in, hid, of_group(g), 512)

    def expert_near_first(g):
        first(rows, eown_in, ehid, slots_of(g), 0)

    def expert_far_first(g):
        first(rows, efar_in, ehid, slots_of(g), 512)

    def dense_near(g):
        def body(cols):
            dense[of_group(g), cols] = jnp.dot(
                hid[of_group(g), 0:512], own_out[:, cols], preferred_element_type=F32
            )

        tiles(2048, body)

    def dense_far(g):
        def body(cols):
            dense[of_group(g), cols] += jnp.dot(
                hid[of_group(g), 512:1024], far_out[:, cols], preferred_element_type=F32
            )

        tiles(2048, body)

    def expert_second(g):
        def body(cols):
            near, far = ehid[slots_of(g), 0:512], ehid[slots_of(g), 512:1024]
            got = jnp.dot(near, eown_out[:, cols], preferred_element_type=F32)
            got += jnp.dot(far, efar_out[:, cols], preferred_element_type=F32)
            got = got.astype(BF16)
            back[slot_rows(g, 0), cols] = got[0 : SLOTS[g]]
            leaving[pl.ds(PICKED_AT[g], 3 * SLOTS[g]), cols] = got[SLOTS[g] :]

        tiles(2048, body)

    def give_back(g):
        for k in (2, 3, 1):
            send(
                leaving.at[picked_rows(g, k)], back.at[slot_rows(g, k)],
                ret_s.at[g, k], ret_r.at[g, k], peer(g, -k),
            )

    def combine(g):
        for k in (1, 2, 3):
            arrived(back.at[slot_rows(g, k)], ret_s.at[g, k], ret_r.at[g, k], peer(g, k))
        put = weighting(g)

        def body(cols):
            dense[of_group(g), cols] += jnp.dot(
                put, back[slots_of(g), cols], preferred_element_type=F32
            )

        tiles(2048, body)

    for copy in local:
        copy.wait()
    hop_in(1, 0)
    leg2(2)
    leg1(3)
    hop_in(1, 1)
    leg2(4)
    leg1(5)
    dense_near_first(0)
    leg3(2)
    hop_in(2, 0)
    leg2(3)
    leg3(4)
    hop_in(2, 1)
    leg2(5)
    leg2(0)
    direct()
    dispatch(0)
    leg4(2)
    hop_in(3, 0)
    leg3(3)
    leg4(4)
    dense_near(0)
    hop_in(3, 1)
    dispatch(2)
    leg3(5)
    dense_near_first(2)
    hop_in(4, 0)
    dispatch(3)
    leg4(3)
    dense_near(2)
    dispatched(2)
    expert_near_first(2)
    expert_far_first(2)
    leg4(5)
    leg3(0)
    expert_second(2)
    give_back(2)
    direct_in()
    to_other_core(0)
    dispatch(1)
    leg4(0)
    to_other_core(1)
    dispatched(3)
    expert_near_first(3)
    expert_far_first(3)
    expert_second(3)
    from_other_core(0)
    dense_far_first(2)
    dense_near_first(3)
    from_other_core(1)
    dense_far(2)

    def passing(direction, hop, c):
        return pl.ds(block(1 - direction, hop) + c * HALF, HALF)

    def hop_back(hop, i):
        for direction in range(2):
            c = chunks(direction)[i]
            mine = rs_out.at[direction, hop - 1, pl.ds(c * HALF, HALF)]
            total = dense[passing(direction, hop, c), :]
            if hop < 3 or (hop == 3 and i == 0):
                before = rs_in.at[direction, hop, pl.ds(c * HALF, HALF)]
                arrived(
                    before, rs_s.at[direction, hop, c], rs_r.at[direction, hop, c],
                    along_z(-step[direction]),
                )
                total = total + before[...].astype(F32)
            mine[...] = total.astype(BF16)
            send(
                mine, rs_in.at[direction, hop - 1, pl.ds(c * HALF, HALF)],
                rs_s.at[direction, hop - 1, c], rs_r.at[direction, hop - 1, c],
                along_z(step[direction]),
            )

    combine(2)
    give_back(3)
    hop_back(3, 1)
    dense_far_first(3)
    dense_near(3)
    dense_far(3)
    dispatched(1)
    expert_near_first(1)
    expert_far_first(1)
    expert_second(1)
    give_back(1)
    combine(3)
    hop_back(4, 0)
    dispatched(0)
    expert_near_first(0)
    expert_far_first(0)
    expert_second(0)
    give_back(0)
    dense_near_first(1)
    dense_near(1)
    dense_far_first(1)
    dense_far(1)
    hop_back(3, 0)
    combine(1)
    hop_back(2, 1)
    dense_far_first(0)
    hop_back(2, 0)
    dense_far(0)
    combine(0)
    hop_back(1, 1)
    hop_back(1, 0)
    for c in range(2):
        part = pl.ds(c * HALF, HALF)
        total = dense[part, :]
        for direction in (c, 1 - c):
            before = rs_in.at[direction, 0, part]
            arrived(
                before, rs_s.at[direction, 0, c], rs_r.at[direction, 0, c], along_z(-step[direction])
            )
            total = total + before[...].astype(F32)
        out_ref[part, :] = total.astype(BF16)

    for copy in sent:
        copy.wait_send()


def solution(mesh):
    def shards(inbound, expert_ids, gates, w_in, w_out, mlp_in, mlp_out):
        vmem, dma = pltpu.VMEM, pltpu.SemaphoreType.DMA
        return pl.pallas_call(
            relayed_experts,
            out_shape=jax.ShapeDtypeStruct((ROWS, 2048), BF16),
            in_specs=[pl.BlockSpec(memory_space=pltpu.VMEM)] * 2
            + [pl.BlockSpec(memory_space=pl.ANY)] * 5,
            out_specs=pl.BlockSpec(memory_space=pltpu.VMEM),
            scratch_shapes=[
                vmem((2048, 512), BF16), vmem((512, 2048), BF16),
                vmem((2048, 512), BF16), vmem((512, 2048), BF16),
                vmem((2048, 512), BF16), vmem((512, 2048), BF16),
                vmem((2048, 512), BF16), vmem((512, 2048), BF16),
                vmem((8 * ROWS, 2048), BF16),
                vmem((8, 8, ROWS), F32),
                vmem((3 * sum(SLOTS), 2048), BF16),
                vmem((4 * sum(SLOTS), 2048), BF16),
                vmem((8 * ROWS, 1024), BF16),
                vmem((4 * sum(SLOTS), 1024), BF16),
                vmem((8 * ROWS, 2048), F32),
                vmem((3 * sum(SLOTS), 2048), BF16),
                vmem((4 * sum(SLOTS), 2048), BF16),
                vmem((2, 4, ROWS, 2048), BF16),
                vmem((2, 4, ROWS, 2048), BF16),
                dma((4,)),
                dma((2,)), dma((2,)),
                dma((8,)), dma((8,)),
                dma((2, 4, 2)), dma((2, 4, 2)),
                dma((6,)), dma((6,)),
                dma((6, 4)), dma((6, 4)),
                dma((2,)), dma((2,)),
                dma((4, 4)), dma((4, 4)),
                dma((4, 4)), dma((4, 4)),
                dma((2, 4, 2)), dma((2, 4, 2)),
            ],
            compiler_params=pltpu.CompilerParams(
                collective_id=0, has_side_effects=True, vmem_limit_bytes=60 * 2**20
            ),
        )(
            expert_ids.reshape(1, ROWS), gates.reshape(1, ROWS), inbound,
            w_in[0], w_out[0], mlp_in, mlp_out,
        )

    return jax.shard_map(
        shards,
        mesh=mesh,
        in_specs=(
            P(("section", "dp", "expert"), None),
            P(("section", "dp", "expert"), None),
            P(("section", "dp", "expert"), None),
            P("section", None, "expert"),
            P("section", "expert", None),
            P(None, "expert"),
            P("expert", None),
        ),
        out_specs=P(("section", "dp", "expert"), None),
        check_vma=False,
    )
```

```python
import functools

import jax
import jax.numpy as jnp
from jax import lax
from jax.experimental import pallas as pl
from jax.experimental.pallas import tpu as pltpu
from jax.sharding import PartitionSpec as P

MESH = pl.DeviceIdType.MESH
F32 = jnp.float32
BF16 = jnp.bfloat16
ROWS = 128
HALF = 64
CAP = 20
BLOCKS = ((0, 1, 7), (2, 6), (3, 5), (4,))
TOKENS = tuple(len(group) * ROWS for group in BLOCKS)
TOKENS_AT = tuple(sum(TOKENS[:g]) for g in range(4))
SLOTS = (64, 48, 48, 32)
SLOTS_AT = tuple(4 * sum(SLOTS[:g]) for g in range(4))
PICKED_AT = tuple(3 * sum(SLOTS[:g]) for g in range(4))
FAR_SIDE = (1,)
BLOCK_AT = {k: TOKENS_AT[g] + i * ROWS for g in range(4) for i, k in enumerate(BLOCKS[g])}
COLS = 1024


def relayed_experts(
    ids_ref, gates_ref, inbound, w_in, w_out, mlp_in, mlp_out, out_ref,
    own_in, own_out, far_in, far_out, eown_in, eown_out, efar_in, efar_out,
    x, info, picked, rows, hid, ehid, dense, leaving, back, rs_out, rs_in,
    local_sem, hand_s, hand_r, info_s, info_r, ag_s, ag_r, w1_s, w1_r, w2_s, w2_r,
    core_s, core_r, disp_s, disp_r, ret_s, ret_r, rs_s, rs_r,
):
    s, d, e = lax.axis_index("section"), lax.axis_index("dp"), lax.axis_index("expert")
    core = lax.rem(s, 2)
    flip_e = e + 1 - 2 * lax.rem(e, 2)

    def along_z(k):
        return (s, d, lax.rem(e + 2 * (k % 8), 16))

    def at_section(k):
        return (lax.rem(s + k % 4, 4), d, e)

    def peer(g, k):
        t, _, _ = at_section(k)
        if g in FAR_SIDE:
            return (t, d, jnp.where(t // 2 == s // 2, e, flip_e))
        return (t, d, e)

    def along_x(k):
        return (s, lax.rem(d + k % 4, 4), e)

    other_core = (s + 1 - 2 * core, d, e)
    far_expert = (s, d, flip_e)
    far_mlp = (lax.rem(s + 2, 4), d, flip_e)

    barrier = pltpu.get_barrier_semaphore()
    partners = [along_z(k) for k in range(1, 8)] + [at_section(k) for k in (1, 2, 3)]
    partners += [(lax.rem(s + 3 - 2 * core, 4), d, flip_e), along_x(1), along_x(3), far_expert, far_mlp]
    for partner in partners:
        pl.semaphore_signal(barrier, inc=1, device_id=partner, device_id_type=MESH)

    local = [
        pltpu.make_async_copy(src, dst, local_sem.at[i])
        for i, (src, dst) in enumerate(
            [(mlp_in, own_in), (mlp_out, own_out), (w_in, eown_in), (w_out, eown_out)]
        )
    ]
    for copy in local:
        copy.start()
    pl.semaphore_wait(barrier, len(partners))

    sent = []

    def send(src, dst, send_sem, recv_sem, device):
        copy = pltpu.make_async_remote_copy(
            src_ref=src, dst_ref=dst, send_sem=send_sem, recv_sem=recv_sem,
            device_id=device, device_id_type=MESH,
        )
        copy.start()
        sent.append(copy)

    def arrived(dst, send_sem, recv_sem, device):
        pltpu.make_async_remote_copy(
            src_ref=dst, dst_ref=dst, send_sem=send_sem, recv_sem=recv_sem,
            device_id=device, device_id_type=MESH,
        ).wait_recv()

    for c in range(2):
        part = pl.ds(c * HALF, HALF)
        send(inbound.at[part], x.at[part], hand_s.at[c], hand_r.at[c], at_section(1))

    streams = [
        (mlp_out, far_out, 64, core * 256, far_mlp),
        None,
        (w_in, efar_in, 256, 0, far_expert),
        (w_out, efar_out, 64, 0, far_expert),
        (w_in, efar_in, 256, 1024, far_expert),
        (w_out, efar_out, 64, 256, far_expert),
    ]

    def quarter(i, ref, k, part=None):
        _, _, q, base, _ = streams[i]
        first = base + lax.rem(d + k % 4, 4) * q
        if part is None:
            return ref.at[pl.ds(pl.multiple_of(first, 64), q)]
        return ref.at[pl.ds(pl.multiple_of(first + part * (q // 2), 32), q // 2)]

    def leg1(i):
        src, dst, _, _, device = streams[i]
        send(quarter(i, src, 0), quarter(i, dst, 0), w1_s.at[i], w1_r.at[i], device)

    def leg2(i):
        dst, device = streams[i][1], streams[i][4]
        mine = quarter(i, dst, 0)
        arrived(mine, w1_s.at[i], w1_r.at[i], device)
        send(mine, mine, w2_s.at[i, 0], w2_r.at[i, 0], along_x(1))
        send(mine, mine, w2_s.at[i, 1], w2_r.at[i, 1], along_x(3))

    def leg3(i):
        dst = streams[i][1]
        arrived(quarter(i, dst, 3), w2_s.at[i, 0], w2_r.at[i, 0], along_x(3))
        part = quarter(i, dst, 3, 0)
        send(part, part, w2_s.at[i, 2], w2_r.at[i, 2], along_x(1))
        arrived(quarter(i, dst, 1), w2_s.at[i, 1], w2_r.at[i, 1], along_x(1))
        part = quarter(i, dst, 1, 1)
        send(part, part, w2_s.at[i, 3], w2_r.at[i, 3], along_x(3))

    def leg4(i):
        dst = streams[i][1]
        arrived(quarter(i, dst, 2, 0), w2_s.at[i, 2], w2_r.at[i, 2], along_x(3))
        arrived(quarter(i, dst, 2, 1), w2_s.at[i, 3], w2_r.at[i, 3], along_x(1))

    def mlp_half(i, ref, side):
        n = (1024, 256)[i]
        return ref.at[pl.ds(pl.multiple_of(side * n, 64), n)]

    def direct():
        src, dst = mlp_half(0, mlp_in, core), mlp_half(0, far_in, core)
        send(src, dst, w1_s.at[1], w1_r.at[1], far_mlp)

    def direct_in():
        arrived(mlp_half(0, far_in, core), w1_s.at[1], w1_r.at[1], far_mlp)

    def to_other_core(i):
        half = mlp_half(i, (far_in, far_out)[i], core)
        send(half, half, core_s.at[i], core_r.at[i], other_core)

    def from_other_core(i):
        arrived(mlp_half(i, (far_in, far_out)[i], 1 - core), core_s.at[i], core_r.at[i], other_core)

    leg1(0)

    ids = jnp.broadcast_to(ids_ref[...].astype(F32), (ROWS, ROWS))
    earlier = lax.broadcasted_iota(jnp.int32, (ROWS, ROWS), 0)
    token = lax.broadcasted_iota(jnp.int32, (ROWS, ROWS), 1)
    same = jnp.where((ids.T == ids) & (earlier < token), 1.0, 0.0)
    position = jnp.sum(same, axis=0, keepdims=True)
    relative = ids_ref[...] - s
    relative = jnp.where(relative < 0, relative + 4, relative).astype(F32)
    position = jnp.where(position < CAP, position, -1e6)
    line = lax.broadcasted_iota(jnp.int32, (8, ROWS), 0)
    info[0] = jnp.where(
        line == 0,
        jnp.broadcast_to(relative, (8, ROWS)),
        jnp.where(
            line == 1,
            jnp.broadcast_to(position, (8, ROWS)),
            jnp.broadcast_to(gates_ref[...], (8, ROWS)),
        ),
    )
    for k in range(1, 8):
        send(info.at[0], info.at[k], info_s.at[k], info_r.at[k], along_z(k))

    step = (1, -1)

    def block(direction, hop):
        return BLOCK_AT[hop if direction == 0 else 8 - hop]

    def place(direction, hop, c):
        return x.at[pl.ds(block(direction, hop) + c * HALF, HALF)]

    def chunks(direction):
        return (0, 1) if direction == 0 else (1, 0)

    def hop_out(direction, hop, c, src):
        send(
            src, place(direction, hop, c),
            ag_s.at[direction, hop - 1, c], ag_r.at[direction, hop - 1, c],
            along_z(step[direction]),
        )

    def hop_in(hop, i):
        for direction in range(2):
            c = chunks(direction)[i]
            dst = place(direction, hop, c)
            arrived(
                dst, ag_s.at[direction, hop - 1, c], ag_r.at[direction, hop - 1, c],
                along_z(-step[direction]),
            )
            if hop < 3 or (hop == 3 and i == 0):
                hop_out(direction, hop + 1, c, dst)

    for c in range(2):
        own = x.at[pl.ds(c * HALF, HALF)]
        arrived(own, hand_s.at[c], hand_r.at[c], at_section(3))
        for direction in range(2):
            hop_out(direction, 1, c, own)
        leg1((2, 4)[c])

    def placing(g):
        parts = []
        for side, k in enumerate(BLOCKS[g]):
            slot = lax.broadcasted_iota(jnp.int32, (4 * SLOTS[g], ROWS), 0).astype(F32)
            want = info[k, 0:1, :] * float(SLOTS[g]) + info[k, 1:2, :] + float(side * CAP)
            parts.append(jnp.where(slot == want, 1.0, 0.0))
        return jnp.concatenate(parts, axis=1).astype(BF16)

    def weighting(g):
        parts = []
        for side, k in enumerate(BLOCKS[g]):
            columns = info[k].T
            slot = lax.broadcasted_iota(jnp.int32, (ROWS, 4 * SLOTS[g]), 1).astype(F32)
            want = columns[:, 0:1] * float(SLOTS[g]) + columns[:, 1:2] + float(side * CAP)
            parts.append(jnp.where(slot == want, columns[:, 2:3], 0.0))
        return jnp.concatenate(parts, axis=0).astype(BF16)

    def of_group(g):
        return pl.ds(TOKENS_AT[g], TOKENS[g])

    def slots_of(g):
        return pl.ds(SLOTS_AT[g], 4 * SLOTS[g])

    def slot_rows(g, k):
        return pl.ds(SLOTS_AT[g] + k * SLOTS[g], SLOTS[g])

    def picked_rows(g, k):
        return pl.ds(PICKED_AT[g] + (k - 1) * SLOTS[g], SLOTS[g])

    def tiles(n, body):
        def run(i, _):
            body(pl.ds(pl.multiple_of(i * COLS, COLS), COLS))
            return 0

        lax.fori_loop(0, n // COLS, run, 0)

    def dispatch(g):
        for k in BLOCKS[g]:
            if k:
                arrived(info.at[k], info_s.at[k], info_r.at[k], along_z(-k))
        pick = placing(g)

        def body(cols):
            got = jnp.dot(pick, x[of_group(g), cols], preferred_element_type=F32).astype(BF16)
            rows[slot_rows(g, 0), cols] = got[0 : SLOTS[g]]
            picked[pl.ds(PICKED_AT[g], 3 * SLOTS[g]), cols] = got[SLOTS[g] :]

        tiles(2048, body)
        for k in (2, 3, 1):
            send(
                picked.at[picked_rows(g, k)], rows.at[slot_rows(g, k)],
                disp_s.at[g, k], disp_r.at[g, k], peer(g, k),
            )

    def dispatched(g):
        for k in (1, 2, 3):
            arrived(rows.at[slot_rows(g, k)], disp_s.at[g, k], disp_r.at[g, k], peer(g, -k))

    def first(src, weight, dst, where, offset):
        dst[where, offset : offset + 512] = jax.nn.gelu(
            jnp.dot(src[where, :], weight[...], preferred_element_type=F32), approximate=True
        ).astype(BF16)

    def dense_near_first(g):
        first(x, own_in, hid, of_group(g), 0)

    def dense_far_first(g):
        first(x, far_in, hid, of_group(g), 512)

    def expert_near_first(g):
        first(rows, eown_in, ehid, slots_of(g), 0)

    def expert_far_first(g):
        first(rows, efar_in, ehid, slots_of(g), 512)

    def dense_near(g):
        def body(cols):
            dense[of_group(g), cols] = jnp.dot(
                hid[of_group(g), 0:512], own_out[:, cols], preferred_element_type=F32
            )

        tiles(2048, body)

    def dense_far(g):
        def body(cols):
            dense[of_group(g), cols] += jnp.dot(
                hid[of_group(g), 512:1024], far_out[:, cols], preferred_element_type=F32
            )

        tiles(2048, body)

    def expert_second(g):
        def body(cols):
            near, far = ehid[slots_of(g), 0:512], ehid[slots_of(g), 512:1024]
            got = jnp.dot(near, eown_out[:, cols], preferred_element_type=F32)
            got += jnp.dot(far, efar_out[:, cols], preferred_element_type=F32)
            got = got.astype(BF16)
            back[slot_rows(g, 0), cols] = got[0 : SLOTS[g]]
            leaving[pl.ds(PICKED_AT[g], 3 * SLOTS[g]), cols] = got[SLOTS[g] :]

        tiles(2048, body)

    def give_back(g):
        for k in (2, 3, 1):
            send(
                leaving.at[picked_rows(g, k)], back.at[slot_rows(g, k)],
                ret_s.at[g, k], ret_r.at[g, k], peer(g, -k),
            )

    def combine(g):
        for k in (1, 2, 3):
            arrived(back.at[slot_rows(g, k)], ret_s.at[g, k], ret_r.at[g, k], peer(g, k))
        put = weighting(g)

        def body(cols):
            dense[of_group(g), cols] += jnp.dot(
                put, back[slots_of(g), cols], preferred_element_type=F32
            )

        tiles(2048, body)

    for copy in local:
        copy.wait()
    hop_in(1, 0)
    leg2(2)
    leg1(3)
    hop_in(1, 1)
    leg2(4)
    leg1(5)
    direct()
    dense_near_first(0)
    leg3(2)
    hop_in(2, 0)
    leg2(3)
    leg3(4)
    hop_in(2, 1)
    leg2(5)
    leg2(0)
    dispatch(0)
    leg4(2)
    hop_in(3, 0)
    leg3(3)
    leg4(4)
    dense_near(0)
    hop_in(3, 1)
    dispatch(2)
    leg3(5)
    dense_near_first(2)
    hop_in(4, 0)
    dispatch(3)
    leg4(3)
    dense_near(2)
    dispatched(2)
    expert_near_first(2)
    expert_far_first(2)
    leg4(5)
    leg3(0)
    expert_second(2)
    give_back(2)
    direct_in()
    to_other_core(0)
    dispatch(1)
    leg4(0)
    to_other_core(1)
    dispatched(3)
    expert_near_first(3)
    expert_far_first(3)
    expert_second(3)
    from_other_core(0)
    dense_far_first(2)
    dense_near_first(3)
    from_other_core(1)
    dense_far(2)

    def passing(direction, hop, c):
        return pl.ds(block(1 - direction, hop) + c * HALF, HALF)

    def hop_back(hop, i):
        for direction in range(2):
            c = chunks(direction)[i]
            mine = rs_out.at[direction, hop - 1, pl.ds(c * HALF, HALF)]
            total = dense[passing(direction, hop, c), :]
            if hop < 3 or (hop == 3 and i == 0):
                before = rs_in.at[direction, hop, pl.ds(c * HALF, HALF)]
                arrived(
                    before, rs_s.at[direction, hop, c], rs_r.at[direction, hop, c],
                    along_z(-step[direction]),
                )
                total = total + before[...].astype(F32)
            mine[...] = total.astype(BF16)
            send(
                mine, rs_in.at[direction, hop - 1, pl.ds(c * HALF, HALF)],
                rs_s.at[direction, hop - 1, c], rs_r.at[direction, hop - 1, c],
                along_z(step[direction]),
            )

    combine(2)
    give_back(3)
    hop_back(3, 1)
    dense_far_first(3)
    dense_near(3)
    dense_far(3)
    dispatched(1)
    expert_near_first(1)
    expert_far_first(1)
    expert_second(1)
    give_back(1)
    combine(3)
    hop_back(4, 0)
    dispatched(0)
    expert_near_first(0)
    expert_far_first(0)
    expert_second(0)
    give_back(0)
    dense_near_first(1)
    dense_near(1)
    dense_far_first(1)
    dense_far(1)
    hop_back(3, 0)
    combine(1)
    hop_back(2, 1)
    dense_far_first(0)
    hop_back(2, 0)
    dense_far(0)
    combine(0)
    hop_back(1, 1)
    hop_back(1, 0)
    for c in range(2):
        part = pl.ds(c * HALF, HALF)
        total = dense[part, :]
        for direction in (c, 1 - c):
            before = rs_in.at[direction, 0, part]
            arrived(
                before, rs_s.at[direction, 0, c], rs_r.at[direction, 0, c], along_z(-step[direction])
            )
            total = total + before[...].astype(F32)
        out_ref[part, :] = total.astype(BF16)

    for copy in sent:
        copy.wait_send()


def solution(mesh):
    def shards(inbound, expert_ids, gates, w_in, w_out, mlp_in, mlp_out):
        vmem, dma = pltpu.VMEM, pltpu.SemaphoreType.DMA
        return pl.pallas_call(
            relayed_experts,
            out_shape=jax.ShapeDtypeStruct((ROWS, 2048), BF16),
            in_specs=[pl.BlockSpec(memory_space=pltpu.VMEM)] * 2
            + [pl.BlockSpec(memory_space=pl.ANY)] * 5,
            out_specs=pl.BlockSpec(memory_space=pltpu.VMEM),
            scratch_shapes=[
                vmem((2048, 512), BF16), vmem((512, 2048), BF16),
                vmem((2048, 512), BF16), vmem((512, 2048), BF16),
                vmem((2048, 512), BF16), vmem((512, 2048), BF16),
                vmem((2048, 512), BF16), vmem((512, 2048), BF16),
                vmem((8 * ROWS, 2048), BF16),
                vmem((8, 8, ROWS), F32),
                vmem((3 * sum(SLOTS), 2048), BF16),
                vmem((4 * sum(SLOTS), 2048), BF16),
                vmem((8 * ROWS, 1024), BF16),
                vmem((4 * sum(SLOTS), 1024), BF16),
                vmem((8 * ROWS, 2048), F32),
                vmem((3 * sum(SLOTS), 2048), BF16),
                vmem((4 * sum(SLOTS), 2048), BF16),
                vmem((2, 4, ROWS, 2048), BF16),
                vmem((2, 4, ROWS, 2048), BF16),
                dma((4,)),
                dma((2,)), dma((2,)),
                dma((8,)), dma((8,)),
                dma((2, 4, 2)), dma((2, 4, 2)),
                dma((6,)), dma((6,)),
                dma((6, 4)), dma((6, 4)),
                dma((2,)), dma((2,)),
                dma((4, 4)), dma((4, 4)),
                dma((4, 4)), dma((4, 4)),
                dma((2, 4, 2)), dma((2, 4, 2)),
            ],
            compiler_params=pltpu.CompilerParams(
                collective_id=0, has_side_effects=True, vmem_limit_bytes=60 * 2**20
            ),
        )(
            expert_ids.reshape(1, ROWS), gates.reshape(1, ROWS), inbound,
            w_in[0], w_out[0], mlp_in, mlp_out,
        )

    return jax.shard_map(
        shards,
        mesh=mesh,
        in_specs=(
            P(("section", "dp", "expert"), None),
            P(("section", "dp", "expert"), None),
            P(("section", "dp", "expert"), None),
            P("section", None, "expert"),
            P("section", "expert", None),
            P(None, "expert"),
            P("expert", None),
        ),
        out_specs=P(("section", "dp", "expert"), None),
        check_vma=False,
    )
```
